768 devices in a mesh: ta: 32 (over z_lo, y), sa: 24 (over z_hi, x, core).
Axes of the slice: x: 4, y: 8, z: 12 (z_hi: 3, z_lo: 4; z = z_hi * 4 + z_lo), core: 2. Of those that a mesh axis runs over, the one named last changes fastest.
Arguments:
- source_field: bfloat16 [2, 3, 4, 32, 32, 24, 128], P(None, None, None, None, 'ta', 'sa'), may hold values from -6 to 6
- gauge_links: bfloat16 [2, 4, 3, 3, 32, 24, 128], P(None, None, None, None, 'ta', 'sa'), may hold values from -6 to 6
- clover: bfloat16 [2, 2, 3, 3, 32, 24, 128], P(None, None, None, None, 'ta', 'sa'), may hold values from -4 to 4
- eigenvectors: bfloat16 [2, 3, 64, 32, 24, 128], P(None, None, None, 'ta', 'sa'), may hold values from -0.046875 to 0.046875
Outputs:
- result_field: bfloat16 [2, 3, 4, 32, 32, 24, 128], P(None, None, None, None, 'ta', 'sa')
- perambulator: float32 [2, 32, 64, 128], P(None, 'ta')
The draws below stay inside these ranges and needn't reach their ends.
All inputs are finite; a program needn't handle non-finite values.
Results may differ from the reference program's by a relative error of at most 0.0045.
Values may be sent and summed in bfloat16 or wider, within the bound.
No kernel may reach another device: no remote copies, remote signals or barrier semaphores. Data moves between devices by JAX's collectives and lax.ppermute only.
A program may use at most 32 MiB of HBM per device.

```python
import jax
import jax.numpy as jnp
from jax import lax

NCOL = 32
NEV = 64
LY = 16
LX = 8
NT = 32
NZ = 24
NYX = 128


def shard_levels(rng, dims, pieces, smallest, high):
    gain, own = 1.0, jax.random.fold_in(rng, 6)
    for axis_at, blocks in pieces:
        steps = jnp.exp(jax.random.uniform(jax.random.fold_in(own, axis_at), (blocks,), jnp.float32, smallest / len(pieces), high / len(pieces)))
        gain = gain * jnp.repeat(steps, dims[axis_at] // blocks).reshape([-1 if axis == axis_at else 1 for axis in range(len(dims))])
    return gain


def noise(key, dims, spread, reach, shards=(), kind=jnp.bfloat16):
    entries = spread * jax.random.normal(key, dims, jnp.float32)
    if shards:
        entries = entries * shard_levels(key, dims, shards, -0.22, 0.18)
    return jnp.clip(entries, -reach, reach).astype(kind)


def setup_inputs(seed: int = 0) -> dict:
    seeds = jax.random.split(jax.random.key(seed), 5)
    return {
        "source_field": noise(seeds[0], (2, 3, 4, NCOL, NT, NZ, NYX), 1.0, 6.0, ((4, 32), (5, 24))),
        "gauge_links": noise(seeds[1], (2, 4, 3, 3, NT, NZ, NYX), 0.4, 6.0, ((4, 32), (5, 24))),
        "clover": noise(seeds[2], (2, 2, 3, 3, NT, NZ, NYX), 0.25, 4.0, ((4, 32), (5, 24))),
        "eigenvectors": noise(seeds[3], (2, 3, NEV, NT, NZ, NYX), (6 * NZ * NYX) ** -0.5, 0.046875, ((3, 32), (4, 24))),
    }


SPIN_REAL = [[[0, 0], [0, 0]], [[0, -1], [1, 0]], [[0, 0], [0, 0]], [[1, 0], [0, 1]]]
SPIN_IMAG = [[[0, -1], [-1, 0]], [[0, 0], [0, 0]], [[-1, 0], [0, 1]], [[0, 0], [0, 0]]]
KAPPA = 0.125


def spin_apply(field, direction, dagger):
    real_tab = SPIN_REAL[direction]
    imag_tab = SPIN_IMAG[direction]
    rows = []
    for s in range(2):
        sum_real = 0.0
        sum_imag = 0.0
        for t in range(2):
            if dagger:
                factor_re = real_tab[t][s]
                factor_im = -imag_tab[t][s]
            else:
                factor_re = real_tab[s][t]
                factor_im = imag_tab[s][t]
            part_re = field[0, :, t]
            part_im = field[1, :, t]
            if factor_re != 0:
                sum_real = sum_real + factor_re * part_re
                sum_imag = sum_imag + factor_re * part_im
            if factor_im != 0:
                sum_real = sum_real - factor_im * part_im
                sum_imag = sum_imag + factor_im * part_re
        rows.append(jnp.stack([sum_real, sum_imag]))
    return jnp.stack(rows, axis=2)


def half_minus(field, direction):
    spins = field.astype(jnp.float32)
    return (spins[:, :, 0:2] - spin_apply(spins[:, :, 2:4], direction, False)).astype(jnp.bfloat16)


def half_plus(field, direction):
    spins = field.astype(jnp.float32)
    return spins[:, :, 0:2] + spin_apply(spins[:, :, 2:4], direction, False)


def rebuild_minus(part, direction):
    return jnp.concatenate([part, -spin_apply(part, direction, True)], axis=2)


def rebuild_plus(part, direction):
    return jnp.concatenate([part, spin_apply(part, direction, True)], axis=2)


def color_apply(links, part, dagger):
    link_re = links[0].astype(jnp.float32)
    link_im = links[1].astype(jnp.float32)
    part = part.astype(jnp.float32)
    out_re = 0.0
    out_im = 0.0
    for b in range(3):
        if dagger:
            coef_re = link_re[b]
            coef_im = -link_im[b]
        else:
            coef_re = link_re[:, b]
            coef_im = link_im[:, b]
        coef_re = coef_re[:, None, None]
        coef_im = coef_im[:, None, None]
        part_re = part[0, b][None]
        part_im = part[1, b][None]
        out_re = out_re + coef_re * part_re - coef_im * part_im
        out_im = out_im + coef_re * part_im + coef_im * part_re
    return jnp.stack([out_re, out_im])


def roll_site(field, direction, amount):
    if direction == 2:
        return jnp.roll(field, amount, axis=-2)
    shape = field.shape
    grid = field.reshape(shape[:-1] + (LY, LX))
    axis_pick = -1 if direction == 0 else -2
    return jnp.roll(grid, amount, axis=axis_pick).reshape(shape)


def clover_apply(clover, field):
    spins = field.astype(jnp.float32)
    upper = spins[:, :, 0:2]
    lower = spins[:, :, 2:4]
    upper = upper + color_apply(clover[:, 0], upper, False)
    lower = lower + color_apply(clover[:, 1], lower, False)
    return jnp.concatenate([upper, lower], axis=2)


def reference(source_field, gauge_links, clover, eigenvectors):
    def one_slice(tslice):
        nxt = ((tslice + 1) % NT).astype(jnp.int32)
        prev = ((tslice + NT - 1) % NT).astype(jnp.int32)
        here = lax.dynamic_index_in_dim(source_field, tslice, axis=4, keepdims=False)
        after = lax.dynamic_index_in_dim(source_field, nxt, axis=4, keepdims=False)
        before = lax.dynamic_index_in_dim(source_field, prev, axis=4, keepdims=False)
        links_here = lax.dynamic_index_in_dim(gauge_links, tslice, axis=4, keepdims=False)
        links_prev = lax.dynamic_index_in_dim(gauge_links, prev, axis=4, keepdims=False)
        clover_here = lax.dynamic_index_in_dim(clover, tslice, axis=4, keepdims=False)
        sign_next = jnp.where(tslice == NT - 1, -1.0, 1.0).astype(jnp.float32)
        sign_prev = jnp.where(tslice == 0, -1.0, 1.0).astype(jnp.float32)
        hopping = jnp.zeros(here.shape, jnp.float32)
        for direction in range(3):
            link_now = links_here[:, direction]
            minus_part = half_minus(here, direction)
            back_part = color_apply(link_now, half_plus(here, direction), True).astype(jnp.bfloat16)
            ahead = roll_site(minus_part, direction, -1)
            behind = roll_site(back_part, direction, 1)
            hopping = hopping + rebuild_minus(color_apply(link_now, ahead, False), direction)
            hopping = hopping + rebuild_plus(behind.astype(jnp.float32), direction)
        ahead = half_minus(after, 3).astype(jnp.float32) * sign_next
        hopping = hopping + rebuild_minus(color_apply(links_here[:, 3], ahead, False), 3)
        back_part = color_apply(links_prev[:, 3], half_plus(before, 3), True).astype(jnp.bfloat16)
        hopping = hopping + rebuild_plus(back_part.astype(jnp.float32) * sign_prev, 3)
        result = (clover_apply(clover_here, here) - KAPPA * hopping).astype(jnp.bfloat16)
        vectors = lax.dynamic_index_in_dim(eigenvectors, tslice, axis=3, keepdims=False)
        left = vectors.astype(jnp.float32).reshape((6, NEV) + vectors.shape[3:])
        flat = result.astype(jnp.float32).reshape((6, 4 * NCOL) + result.shape[4:])
        swapped = jnp.concatenate([flat[3:], -flat[:3]], axis=0)
        right = jnp.stack([flat, swapped])
        projected = jnp.einsum("rkzx,qrmzx->qkm", left, right)
        return result, projected

    results, projections = lax.map(one_slice, jnp.arange(NT, dtype=jnp.int32))
    return jnp.moveaxis(results, 0, 4), jnp.moveaxis(projections, 0, 1)
```

```python
import functools

import jax
import jax.numpy as jnp
from jax import lax
from jax.experimental import pallas as pl
from jax.experimental.pallas import tpu as pltpu
from jax.sharding import PartitionSpec as P

KAPPA = 0.125
ROWS = 16
F32 = jnp.float32
BF16 = jnp.bfloat16


def add(a, b):
    return (a[0] + b[0], a[1] + b[1])


def sub(a, b):
    return (a[0] - b[0], a[1] - b[1])


def neg(a):
    return (-a[0], -a[1])


def times_i(a):
    return (-a[1], a[0])


def spin(direction, w):
    if direction == 0:
        return [neg(times_i(w[1])), neg(times_i(w[0]))]
    if direction == 1:
        return [neg(w[1]), w[0]]
    if direction == 2:
        return [neg(times_i(w[0])), times_i(w[1])]
    return [w[0], w[1]]


def spin_dagger(direction, w):
    if direction == 0:
        return [times_i(w[1]), times_i(w[0])]
    if direction == 1:
        return [w[1], neg(w[0])]
    if direction == 2:
        return [times_i(w[0]), neg(times_i(w[1]))]
    return [w[0], w[1]]


def rounded(a):
    return (a[0].astype(BF16).astype(F32), a[1].astype(BF16).astype(F32))


def load_field(ref, rows, spins):
    return [
        [(ref[0, c, s, rows, :].astype(F32), ref[1, c, s, rows, :].astype(F32)) for s in range(spins)]
        for c in range(3)
    ]


def load_matrix(ref, which):
    tiles = [[[ref[q, a, b, :, :].astype(F32) for b in range(3)] for a in range(3)] for q in range(2)]
    return [
        [(tiles[0][a][b][which : which + 1, :], tiles[1][a][b][which : which + 1, :]) for b in range(3)]
        for a in range(3)
    ]


def color_row(matrix, part, a, s, dagger):
    re = im = None
    for b in range(3):
        x_re, x_im = part[b][s]
        if dagger:
            m_re, m_im = matrix[b][a]
            terms = (m_re * x_re + m_im * x_im, m_re * x_im - m_im * x_re)
        else:
            m_re, m_im = matrix[a][b]
            terms = (m_re * x_re - m_im * x_im, m_re * x_im + m_im * x_re)
        re = terms[0] if re is None else re + terms[0]
        im = terms[1] if im is None else im + terms[1]
    return (re, im)


def half(field, direction, plus):
    out = []
    for c in range(3):
        turned = spin(direction, [field[c][2], field[c][3]])
        out.append([(add if plus else sub)(field[c][s], turned[s]) for s in range(2)])
    return out


def store_half(ref, rows, part):
    for c in range(3):
        for s in range(2):
            for q in range(2):
                ref[q, c, s, rows, :] = part[c][s][q].astype(BF16)


def edge_kernel(src, links, hz, gz, ht, gt):
    columns = src.shape[3]
    link = {2: load_matrix(links, 2), 3: load_matrix(links, 3)}
    for at in range(0, columns, ROWS):
        rows = pl.ds(at, ROWS)
        field = load_field(src, rows, 4)
        for direction, h_ref, g_ref in ((2, hz, gz), (3, ht, gt)):
            store_half(h_ref, rows, half(field, direction, False))
            plus = half(field, direction, True)
            back = [[color_row(link[direction], plus, a, s, True) for s in range(2)] for a in range(3)]
            store_half(g_ref, rows, back)


def shift_sites(x, direction, ahead):
    lane = lax.broadcasted_iota(jnp.int32, x.shape, 1)
    if direction == 1:
        return pltpu.roll(x, 120 if ahead else 8, 1)
    if ahead:
        return jnp.where(lane % 8 == 7, pltpu.roll(x, 7, 1), pltpu.roll(x, 127, 1))
    return jnp.where(lane % 8 == 0, pltpu.roll(x, 121, 1), pltpu.roll(x, 1, 1))


def local_kernel(src, links, clover, out):
    columns = src.shape[3]
    link = {0: load_matrix(links, 0), 1: load_matrix(links, 1)}
    clov = [load_matrix(clover, 0), load_matrix(clover, 1)]
    for at in range(0, columns, ROWS):
        rows = pl.ds(at, ROWS)
        field = load_field(src, rows, 4)
        hop = [[None] * 4 for _ in range(3)]
        for direction in range(2):
            minus = half(field, direction, False)
            ahead = [
                [tuple(shift_sites(v, direction, True) for v in rounded(minus[c][s])) for s in range(2)]
                for c in range(3)
            ]
            plus = half(field, direction, True)
            for a in range(3):
                w = [color_row(link[direction], ahead, a, s, False) for s in range(2)]
                g = [
                    tuple(
                        shift_sites(v, direction, False)
                        for v in rounded(color_row(link[direction], plus, a, s, True))
                    )
                    for s in range(2)
                ]
                upper = [add(w[s], g[s]) for s in range(2)]
                lower = spin_dagger(direction, [sub(g[s], w[s]) for s in range(2)])
                for s, v in enumerate(upper + lower):
                    hop[a][s] = v if hop[a][s] is None else add(hop[a][s], v)
        for a in range(3):
            for s in range(4):
                own = add(field[a][s], color_row(clov[s // 2], field, a, s, False))
                for q in range(2):
                    out[q, a, s, rows, :] = own[q] - KAPPA * hop[a][s][q]


def finish_kernel(ta_size, local, links, hz, gz, ht, gt, vectors, result, partial):
    columns = local.shape[3]
    me = lax.axis_index("ta")
    ahead_sign = jnp.where(me == ta_size - 1, -1.0, 1.0).astype(F32)
    behind_sign = jnp.where(me == 0, -1.0, 1.0).astype(F32)
    link_z = load_matrix(links, 2)
    link_t = [[(m[0] * ahead_sign, m[1] * ahead_sign) for m in row] for row in load_matrix(links, 3)]
    for at in range(0, columns, ROWS):
        rows = pl.ds(at, ROWS)
        from_z = load_field(hz, rows, 2)
        from_t = load_field(ht, rows, 2)
        back_z = load_field(gz, rows, 2)
        back_t = load_field(gt, rows, 2)
        for a in range(3):
            wz = [color_row(link_z, from_z, a, s, False) for s in range(2)]
            wt = [color_row(link_t, from_t, a, s, False) for s in range(2)]
            gz_now = back_z[a]
            gt_now = [(v[0] * behind_sign, v[1] * behind_sign) for v in back_t[a]]
            lower_z = spin_dagger(2, [sub(gz_now[s], wz[s]) for s in range(2)])
            for s in range(2):
                upper = add(add(wz[s], gz_now[s]), add(wt[s], gt_now[s]))
                lower = add(lower_z[s], sub(gt_now[s], wt[s]))
                for q in range(2):
                    result[q, a, s, rows, :] = (local[q, a, s, rows, :] - KAPPA * upper[q]).astype(BF16)
                    result[q, a, s + 2, rows, :] = (local[q, a, s + 2, rows, :] - KAPPA * lower[q]).astype(BF16)
    total = None
    contract = (((1,), (1,)), ((), ()))
    for c in range(3):
        left_re = vectors[0, c]
        left_im = vectors[1, c]
        for q in range(2):
            right = result[q, c].reshape(4 * columns, result.shape[4])
            left = [left_re, -left_im] if q == 0 else [left_im, left_re]
            term = lax.dot_general(jnp.concatenate(left, axis=0), right, contract, preferred_element_type=F32)
            total = term if total is None else total + term
    partial[...] = total.astype(BF16).reshape(partial.shape)


def call(body, outs, operands, flops):
    vmem = pl.BlockSpec(memory_space=pltpu.VMEM)
    moved = sum(x.size * x.dtype.itemsize for x in list(outs) + list(operands))
    return pl.pallas_call(
        body,
        out_shape=outs,
        in_specs=[vmem] * len(operands),
        out_specs=[vmem] * len(outs),
        compiler_params=pltpu.CompilerParams(vmem_limit_bytes=32 * 2**20),
        cost_estimate=pl.CostEstimate(flops=flops, bytes_accessed=moved, transcendentals=0),
    )(*operands)


def gathered_sum(x, groups):
    both = lax.all_gather(x, "sa", axis_index_groups=groups).astype(F32)
    return lax.reduce_precision(both[0] + both[1], 8, 7).astype(BF16)


def sum_over_blocks(partial, size):
    plane = 8
    planes = size // plane
    cores = [[i, i + 1] for i in range(0, size, 2)]
    starts = range(0, size, plane)
    even = [[z + 4 * p + c, z + 4 * p + 2 + c] for z in starts for p in range(2) for c in range(2)]
    odd = [[z + 2 + c, z + 4 + c] for z in starts for c in range(2)]
    odd += [[z + c, z + 6 + c] for z in starts for c in range(2)]
    s = gathered_sum(partial, cores)
    s = gathered_sum(s, even)
    s = gathered_sum(s, odd)
    pairs = []
    for i in range(size):
        z, r = divmod(i, plane)
        step = 1 if i % 2 else planes - 1
        pairs.append((i, ((z + step) % planes) * plane + r))
    other = lax.all_gather(lax.ppermute(s, "sa", pairs), "sa", axis_index_groups=cores)
    z = lax.axis_index("sa") // plane
    own, nxt, last = s.astype(F32), other[0].astype(F32), other[1].astype(F32)
    first = jnp.where(z == 0, own, jnp.where(z == 1, last, nxt))
    second = jnp.where(z == 0, nxt, jnp.where(z == 1, own, last))
    third = jnp.where(z == 0, last, jnp.where(z == 1, nxt, own))
    return first + second + third


def shards(source_field, gauge_links, clover, eigenvectors):
    sites = source_field.shape[-1]
    columns = source_field.shape[3]
    ta, sa = lax.axis_size("ta"), lax.axis_size("sa")
    src = source_field.reshape(2, 3, 4, columns, sites)
    links = gauge_links.reshape(2, 4, 3, 3, sites).transpose(0, 2, 3, 1, 4)
    clov = clover.reshape(2, 2, 3, 3, sites).transpose(0, 2, 3, 1, 4)
    vectors = eigenvectors.reshape(2, 3, eigenvectors.shape[2], sites)
    half_shape = jax.ShapeDtypeStruct((2, 3, 2, columns, sites), BF16)
    points = columns * sites

    hz, gz, ht, gt = call(edge_kernel, [half_shape] * 4, (src, links), 500 * points)

    def passed(x, axis, size, by):
        return lax.ppermute(x, axis, [(i, (i + by) % size) for i in range(size)])

    hz_in = passed(hz, "sa", sa, -1)
    gz_in = passed(gz, "sa", sa, 1)
    ht_in = passed(ht, "ta", ta, -1)
    gt_in = passed(gt, "ta", ta, 1)
    (local,) = call(
        local_kernel,
        [jax.ShapeDtypeStruct((2, 3, 4, columns, sites), F32)],
        (src, links, clov),
        2000 * points,
    )
    result, partial = call(
        functools.partial(finish_kernel, ta),
        [
            jax.ShapeDtypeStruct((2, 3, 4, columns, sites), BF16),
            jax.ShapeDtypeStruct((2, vectors.shape[2], 4 * columns), BF16),
        ],
        (local, links, hz_in, gz_in, ht_in, gt_in, vectors),
        1000 * points,
    )
    perambulator = sum_over_blocks(partial, sa)
    return result.reshape(source_field.shape), perambulator[:, None]


def solution(mesh):
    in_specs = (
        P(None, None, None, None, "ta", "sa", None),
        P(None, None, None, None, "ta", "sa", None),
        P(None, None, None, None, "ta", "sa", None),
        P(None, None, None, "ta", "sa", None),
    )
    out_specs = (P(None, None, None, None, "ta", "sa", None), P(None, "ta", None, None))
    return jax.shard_map(shards, mesh=mesh, in_specs=in_specs, out_specs=out_specs, check_vma=False)
```

```python
import functools

import jax
import jax.numpy as jnp
from jax import lax
from jax.experimental import pallas as pl
from jax.experimental.pallas import tpu as pltpu
from jax.sharding import PartitionSpec as P

KAPPA = 0.125
ROWS = 16
F32 = jnp.float32
BF16 = jnp.bfloat16


def add(a, b):
    return (a[0] + b[0], a[1] + b[1])


def sub(a, b):
    return (a[0] - b[0], a[1] - b[1])


def neg(a):
    return (-a[0], -a[1])


def times_i(a):
    return (-a[1], a[0])


def spin(direction, w):
    if direction == 0:
        return [neg(times_i(w[1])), neg(times_i(w[0]))]
    if direction == 1:
        return [neg(w[1]), w[0]]
    if direction == 2:
        return [neg(times_i(w[0])), times_i(w[1])]
    return [w[0], w[1]]


def spin_dagger(direction, w):
    if direction == 0:
        return [times_i(w[1]), times_i(w[0])]
    if direction == 1:
        return [w[1], neg(w[0])]
    if direction == 2:
        return [times_i(w[0]), neg(times_i(w[1]))]
    return [w[0], w[1]]


def rounded(a):
    return (a[0].astype(BF16).astype(F32), a[1].astype(BF16).astype(F32))


def load_field(ref, rows, spins):
    return [
        [(ref[0, c, s, rows, :].astype(F32), ref[1, c, s, rows, :].astype(F32)) for s in range(spins)]
        for c in range(3)
    ]


def load_matrix(ref, which):
    tiles = [[[ref[q, a, b, :, :].astype(F32) for b in range(3)] for a in range(3)] for q in range(2)]
    return [
        [(tiles[0][a][b][which : which + 1, :], tiles[1][a][b][which : which + 1, :]) for b in range(3)]
        for a in range(3)
    ]


def color_row(matrix, part, a, s, dagger):
    re = im = None
    for b in range(3):
        x_re, x_im = part[b][s]
        if dagger:
            m_re, m_im = matrix[b][a]
            terms = (m_re * x_re + m_im * x_im, m_re * x_im - m_im * x_re)
        else:
            m_re, m_im = matrix[a][b]
            terms = (m_re * x_re - m_im * x_im, m_re * x_im + m_im * x_re)
        re = terms[0] if re is None else re + terms[0]
        im = terms[1] if im is None else im + terms[1]
    return (re, im)


def half(field, direction, plus):
    out = []
    for c in range(3):
        turned = spin(direction, [field[c][2], field[c][3]])
        out.append([(add if plus else sub)(field[c][s], turned[s]) for s in range(2)])
    return out


def edge_kernel(ta_size, src_hbm, links_hbm, to_core, to_first, to_second, to_third, src, links, sems):
    copies = [
        pltpu.make_async_copy(src_hbm, src, sems.at[0]),
        pltpu.make_async_copy(links_hbm, links, sems.at[1]),
    ]
    for copy in copies:
        copy.start()
    for copy in copies:
        copy.wait()
    columns = src.shape[3]
    link_z, link_t = load_matrix(links, 2), load_matrix(links, 3)
    me = lax.axis_index("ta")
    even_z = lax.axis_index("sa") % 2 == 0
    even_t = me % 2 == 0
    last = me >= ta_size - 2
    for at in range(0, columns, ROWS):
        rows = pl.ds(at, ROWS)
        field = load_field(src, rows, 4)
        minus_z, minus_t = half(field, 2, False), half(field, 3, False)
        plus_z, plus_t = half(field, 2, True), half(field, 3, True)
        for a in range(3):
            for s in range(2):
                back_z = color_row(link_z, plus_z, a, s, True)
                back_t = color_row(link_t, plus_t, a, s, True)
                for q in range(2):
                    to_core[q, a, s, rows, :] = jnp.where(even_z, back_z[q], minus_z[a][s][q]).astype(BF16)
                    chip = jnp.where(even_z, minus_z[a][s][q], back_z[q])
                    even = jnp.where(even_t, back_t[q], minus_t[a][s][q])
                    odd = jnp.where(even_t, minus_t[a][s][q], back_t[q])
                    to_first[q, a, s, rows, :] = jnp.where(last, even, chip).astype(BF16)
                    to_second[q, a, s, rows, :] = odd.astype(BF16)
                    to_third[q, a, s, rows, :] = jnp.where(last, chip, even).astype(BF16)


def shift_sites(x, direction, ahead):
    lane = lax.broadcasted_iota(jnp.int32, x.shape, 1)
    if direction == 1:
        return pltpu.roll(x, 120 if ahead else 8, 1)
    if ahead:
        return jnp.where(lane % 8 == 7, pltpu.roll(x, 7, 1), pltpu.roll(x, 127, 1))
    return jnp.where(lane % 8 == 0, pltpu.roll(x, 121, 1), pltpu.roll(x, 1, 1))


def local_kernel(src, links, clover, out):
    columns = src.shape[3]
    link = {0: load_matrix(links, 0), 1: load_matrix(links, 1)}
    clov = [load_matrix(clover, 0), load_matrix(clover, 1)]
    for at in range(0, columns, ROWS):
        rows = pl.ds(at, ROWS)
        field = load_field(src, rows, 4)
        hop = [[None] * 4 for _ in range(3)]
        for direction in range(2):
            minus = half(field, direction, False)
            ahead = [
                [tuple(shift_sites(v, direction, True) for v in rounded(minus[c][s])) for s in range(2)]
                for c in range(3)
            ]
            plus = half(field, direction, True)
            for a in range(3):
                w = [color_row(link[direction], ahead, a, s, False) for s in range(2)]
                g = [
                    tuple(
                        shift_sites(v, direction, False)
                        for v in rounded(color_row(link[direction], plus, a, s, True))
                    )
                    for s in range(2)
                ]
                upper = [add(w[s], g[s]) for s in range(2)]
                lower = spin_dagger(direction, [sub(g[s], w[s]) for s in range(2)])
                for s, v in enumerate(upper + lower):
                    hop[a][s] = v if hop[a][s] is None else add(hop[a][s], v)
        for a in range(3):
            for s in range(4):
                own = add(field[a][s], color_row(clov[s // 2], field, a, s, False))
                for q in range(2):
                    out[q, a, s, rows, :] = own[q] - KAPPA * hop[a][s][q]


def chosen(first, a, b):
    return [[tuple(jnp.where(first, p, q) for p, q in zip(v, w)) for v, w in zip(x, y)] for x, y in zip(a, b)]


def finish_kernel(ta_size, local, links, cores, first, second, third, vectors, result, partial):
    columns = local.shape[3]
    me = lax.axis_index("ta")
    core = lax.axis_index("sa") % 2
    even_z = core == 0
    even_t = me % 2 == 0
    last = me >= ta_size - 2
    ahead_sign = jnp.where(me == ta_size - 1, -1.0, 1.0).astype(F32)
    behind_sign = jnp.where(me == 0, -1.0, 1.0).astype(F32)
    link_z = load_matrix(links, 2)
    link_t = [[(m[0] * ahead_sign, m[1] * ahead_sign) for m in row] for row in load_matrix(links, 3)]
    for at in range(0, columns, ROWS):
        rows = pl.ds(at, ROWS)
        one, three = load_field(first, rows, 2), load_field(third, rows, 2)
        near, far = load_field(cores.at[1 - core], rows, 2), chosen(last, three, one)
        from_z, back_z = chosen(even_z, near, far), chosen(even_z, far, near)
        near, far = chosen(last, one, three), load_field(second, rows, 2)
        from_t, back_t = chosen(even_t, near, far), chosen(even_t, far, near)
        for a in range(3):
            wz = [color_row(link_z, from_z, a, s, False) for s in range(2)]
            wt = [color_row(link_t, from_t, a, s, False) for s in range(2)]
            gz_now = back_z[a]
            gt_now = [(v[0] * behind_sign, v[1] * behind_sign) for v in back_t[a]]
            lower_z = spin_dagger(2, [sub(gz_now[s], wz[s]) for s in range(2)])
            for s in range(2):
                upper = add(add(wz[s], gz_now[s]), add(wt[s], gt_now[s]))
                lower = add(lower_z[s], sub(gt_now[s], wt[s]))
                for q in range(2):
                    result[q, a, s, rows, :] = (local[q, a, s, rows, :] - KAPPA * upper[q]).astype(BF16)
                    result[q, a, s + 2, rows, :] = (local[q, a, s + 2, rows, :] - KAPPA * lower[q]).astype(BF16)
    total = None
    contract = (((1,), (1,)), ((), ()))
    for c in range(3):
        left_re = vectors[0, c]
        left_im = vectors[1, c]
        for q in range(2):
            right = result[q, c].reshape(4 * columns, result.shape[4])
            left = [left_re, -left_im] if q == 0 else [left_im, left_re]
            term = lax.dot_general(jnp.concatenate(left, axis=0), right, contract, preferred_element_type=F32)
            total = term if total is None else total + term
    partial[...] = total.reshape(partial.shape)


def call(body, outs, operands, flops, in_specs=None, scratch_shapes=()):
    vmem = pl.BlockSpec(memory_space=pltpu.VMEM)
    moved = sum(x.size * x.dtype.itemsize for x in list(outs) + list(operands))
    return pl.pallas_call(
        body,
        out_shape=outs,
        in_specs=in_specs or [vmem] * len(operands),
        out_specs=[vmem] * len(outs),
        scratch_shapes=scratch_shapes,
        compiler_params=pltpu.CompilerParams(vmem_limit_bytes=32 * 2**20),
        cost_estimate=pl.CostEstimate(flops=flops, bytes_accessed=moved, transcendentals=0),
    )(*operands)


def gathered_sum(x, groups):
    both = lax.all_gather(x, "sa", axis_index_groups=groups).astype(F32)
    return lax.reduce_precision(both[0] + both[1], 8, 7).astype(BF16)


def sum_over_blocks(partial, size):
    plane = 8
    planes = size // plane
    cores = [[i, i + 1] for i in range(0, size, 2)]
    starts = range(0, size, plane)
    even = [[z + 4 * p + c, z + 4 * p + 2 + c] for z in starts for p in range(2) for c in range(2)]
    odd = [[z + 2 + c, z + 4 + c] for z in starts for c in range(2)]
    odd += [[z + c, z + 6 + c] for z in starts for c in range(2)]
    s = gathered_sum(partial, cores)
    row = [[z + 2 * x + c for x in range(4)] for z in starts for c in range(2)]
    four = lax.all_to_all(jnp.broadcast_to(s[None], (4,) + s.shape), "sa", 0, 0, axis_index_groups=row).astype(F32)
    s = lax.reduce_precision((four[0] + four[1]) + (four[2] + four[3]), 8, 7).astype(BF16)
    pairs = []
    for i in range(size):
        z, r = divmod(i, plane)
        step = 1 if i % 2 else planes - 1
        pairs.append((i, ((z + step) % planes) * plane + r))
    other = lax.all_gather(lax.ppermute(s, "sa", pairs), "sa", axis_index_groups=cores)
    z = lax.axis_index("sa") // plane
    own, nxt, last = s.astype(F32), other[0].astype(F32), other[1].astype(F32)
    first = jnp.where(z == 0, own, jnp.where(z == 1, last, nxt))
    second = jnp.where(z == 0, nxt, jnp.where(z == 1, own, last))
    third = jnp.where(z == 0, last, jnp.where(z == 1, nxt, own))
    return first + second + third


def shards(source_field, gauge_links, clover, eigenvectors):
    sites = source_field.shape[-1]
    columns = source_field.shape[3]
    ta, sa = lax.axis_size("ta"), lax.axis_size("sa")
    src = source_field.reshape(2, 3, 4, columns, sites)
    links = gauge_links.reshape(2, 4, 3, 3, sites).transpose(0, 2, 3, 1, 4)
    clov = clover.reshape(2, 2, 3, 3, sites).transpose(0, 2, 3, 1, 4)
    vectors = eigenvectors.reshape(2, 3, eigenvectors.shape[2], sites)
    half_shape = jax.ShapeDtypeStruct((2, 3, 2, columns, sites), BF16)
    points = columns * sites

    to_core, to_first, to_second, to_third = call(
        functools.partial(edge_kernel, ta),
        [half_shape] * 4,
        (src, links),
        500 * points,
        in_specs=[pl.BlockSpec(memory_space=pl.ANY)] * 2,
        scratch_shapes=[
            pltpu.VMEM(src.shape, BF16),
            pltpu.VMEM(links.shape, BF16),
            pltpu.SemaphoreType.DMA((2,)),
        ],
    )

    def place(t, z):
        return (t % ta) * sa + z % sa

    def along_z(slabs):
        return [(place(t, z), place(t, z + (1 if z % 2 else -1))) for t in slabs for z in range(sa)]

    def along_t(slabs, parity):
        return [(place(t, z), place(t + (1 if t % 2 == parity else -1), z)) for t in slabs for z in range(sa)]

    most, rest = range(ta - 2), range(ta - 2, ta)
    first = lax.ppermute(to_first, ("ta", "sa"), along_z(most) + along_t(rest, 0))
    second = lax.ppermute(to_second, ("ta", "sa"), along_t(range(ta), 1))
    third = lax.ppermute(to_third, ("ta", "sa"), along_t(most, 0) + along_z(rest))
    cores = lax.all_gather(to_core, "sa", axis_index_groups=[[i, i + 1] for i in range(0, sa, 2)])
    (local,) = call(
        local_kernel,
        [jax.ShapeDtypeStruct((2, 3, 4, columns, sites), F32)],
        (src, links, clov),
        2000 * points,
    )
    result, partial = call(
        functools.partial(finish_kernel, ta),
        [
            jax.ShapeDtypeStruct((2, 3, 4, columns, sites), BF16),
            jax.ShapeDtypeStruct((2, vectors.shape[2], 4 * columns), F32),
        ],
        (local, links, cores, first, second, third, vectors),
        1000 * points,
    )
    perambulator = sum_over_blocks(partial, sa)
    return result.reshape(source_field.shape), perambulator[:, None]


def solution(mesh):
    in_specs = (
        P(None, None, None, None, "ta", "sa", None),
        P(None, None, None, None, "ta", "sa", None),
        P(None, None, None, None, "ta", "sa", None),
        P(None, None, None, "ta", "sa", None),
    )
    out_specs = (P(None, None, None, None, "ta", "sa", None), P(None, "ta", None, None))
    return jax.shard_map(shards, mesh=mesh, in_specs=in_specs, out_specs=out_specs, check_vma=False)
```

```python
import functools

import jax
import jax.numpy as jnp
from jax import lax
from jax.experimental import pallas as pl
from jax.experimental.pallas import tpu as pltpu
from jax.sharding import PartitionSpec as P

KAPPA = 0.125
ROWS = 16
LINK_ROWS = 72
F32 = jnp.float32
BF16 = jnp.bfloat16


def add(a, b):
    return (a[0] + b[0], a[1] + b[1])


def sub(a, b):
    return (a[0] - b[0], a[1] - b[1])


def neg(a):
    return (-a[0], -a[1])


def times_i(a):
    return (-a[1], a[0])


def spin(direction, w):
    if direction == 0:
        return [neg(times_i(w[1])), neg(times_i(w[0]))]
    if direction == 1:
        return [neg(w[1]), w[0]]
    if direction == 2:
        return [neg(times_i(w[0])), times_i(w[1])]
    return [w[0], w[1]]


def spin_dagger(direction, w):
    if direction == 0:
        return [times_i(w[1]), times_i(w[0])]
    if direction == 1:
        return [w[1], neg(w[0])]
    if direction == 2:
        return [times_i(w[0]), neg(times_i(w[1]))]
    return [w[0], w[1]]


def rounded(a):
    return (a[0].astype(BF16).astype(F32), a[1].astype(BF16).astype(F32))


def load_field(ref, rows, spins):
    return [
        [(ref[0, c, s, rows, :].astype(F32), ref[1, c, s, rows, :].astype(F32)) for s in range(spins)]
        for c in range(3)
    ]


class Field:
    def __init__(self, packed):
        self.packed, self.shape = packed, (2, 3, 4, (packed.shape[0] - LINK_ROWS) // 24, packed.shape[1])

    def __getitem__(self, at):
        q, c, s, rows, _ = at
        return self.packed[pl.ds(((q * 3 + c) * 4 + s) * self.shape[3] + rows.start, rows.size), :]


def load_links(packed, *directions):
    block = packed[pl.ds(packed.shape[0] - LINK_ROWS, LINK_ROWS), :].astype(F32)

    def row(q, a, b, direction):
        at = ((q * 3 + a) * 3 + b) * 4 + direction
        return block[at : at + 1, :]

    return [
        [[(row(0, a, b, direction), row(1, a, b, direction)) for b in range(3)] for a in range(3)]
        for direction in directions
    ]


def load_matrix(ref, which):
    tiles = [[[ref[q, a, b, :, :].astype(F32) for b in range(3)] for a in range(3)] for q in range(2)]
    return [
        [(tiles[0][a][b][which : which + 1, :], tiles[1][a][b][which : which + 1, :]) for b in range(3)]
        for a in range(3)
    ]


def color_row(matrix, part, a, s, dagger):
    re = im = None
    for b in range(3):
        x_re, x_im = part[b][s]
        if dagger:
            m_re, m_im = matrix[b][a]
            terms = (m_re * x_re + m_im * x_im, m_re * x_im - m_im * x_re)
        else:
            m_re, m_im = matrix[a][b]
            terms = (m_re * x_re - m_im * x_im, m_re * x_im + m_im * x_re)
        re = terms[0] if re is None else re + terms[0]
        im = terms[1] if im is None else im + terms[1]
    return (re, im)


def half(field, direction, plus):
    out = []
    for c in range(3):
        turned = spin(direction, [field[c][2], field[c][3]])
        out.append([(add if plus else sub)(field[c][s], turned[s]) for s in range(2)])
    return out


def edge_kernel(ta_size, packed, to_core, to_first, to_second, to_third):
    src = Field(packed)
    columns = src.shape[3]
    link_z, link_t = load_links(packed, 2, 3)
    me = lax.axis_index("ta")
    even_z = lax.axis_index("sa") % 2 == 0
    even_t = me % 2 == 0
    last = me >= ta_size - 2
    for at in range(0, columns, ROWS):
        rows = pl.ds(at, ROWS)
        field = load_field(src, rows, 4)
        minus_z, minus_t = half(field, 2, False), half(field, 3, False)
        plus_z, plus_t = half(field, 2, True), half(field, 3, True)
        for a in range(3):
            for s in range(2):
                back_z = color_row(link_z, plus_z, a, s, True)
                back_t = color_row(link_t, plus_t, a, s, True)
                for q in range(2):
                    to_core[q, a, s, rows, :] = jnp.where(even_z, back_z[q], minus_z[a][s][q]).astype(BF16)
                    chip = jnp.where(even_z, minus_z[a][s][q], back_z[q])
                    even = jnp.where(even_t, back_t[q], minus_t[a][s][q])
                    odd = jnp.where(even_t, minus_t[a][s][q], back_t[q])
                    to_first[q, a, s, rows, :] = jnp.where(last, even, chip).astype(BF16)
                    to_second[q, a, s, rows, :] = odd.astype(BF16)
                    to_third[q, a, s, rows, :] = jnp.where(last, chip, even).astype(BF16)


def shift_sites(x, direction, ahead):
    lane = lax.broadcasted_iota(jnp.int32, x.shape, 1)
    if direction == 1:
        return pltpu.roll(x, 120 if ahead else 8, 1)
    if ahead:
        return jnp.where(lane % 8 == 7, pltpu.roll(x, 7, 1), pltpu.roll(x, 127, 1))
    return jnp.where(lane % 8 == 0, pltpu.roll(x, 121, 1), pltpu.roll(x, 1, 1))


def add_to(hop, a, values):
    for s, v in enumerate(values):
        hop[a][s] = v if hop[a][s] is None else add(hop[a][s], v)


def place_on_mesh(ta_size):
    me, core = lax.axis_index("ta"), lax.axis_index("sa") % 2
    ahead_sign = jnp.where(me == ta_size - 1, -1.0, 1.0).astype(F32)
    behind_sign = jnp.where(me == 0, -1.0, 1.0).astype(F32)
    return core, me % 2, me >= ta_size - 2, ahead_sign, behind_sign


def chosen_matrix(first, a, b):
    return [[tuple(jnp.where(first, p, q) for p, q in zip(v, w)) for v, w in zip(x, y)] for x, y in zip(a, b)]


def add_swapped(hop, link, part, forward, turn, forward_sign=None, backward_sign=None):
    for a in range(3):
        upper, signed = [], []
        for s in range(2):
            w, g = color_row(link, part, a, s, False), part[a][s]
            if forward_sign is not None:
                w = (w[0] * forward_sign, w[1] * forward_sign)
                g = (g[0] * backward_sign, g[1] * backward_sign)
            upper.append(tuple(jnp.where(forward, p, q) for p, q in zip(w, g)))
            signed.append(tuple(jnp.where(forward, -p, q) for p, q in zip(w, g)))
        add_to(hop, a, upper + turn(signed))


def turned_z(w):
    return spin_dagger(2, w)


def turned_t(w):
    return spin_dagger(3, w)


def turned_either(along_t, w):
    return [
        tuple(jnp.where(along_t, p, q) for p, q in zip(v, u)) for v, u in zip(turned_t(w), turned_z(w))
    ]


def local_kernel(ta_size, packed, clover, cores, first, second, out):
    src = Field(packed)
    columns = src.shape[3]
    core, odd_t, last, ahead_sign, behind_sign = place_on_mesh(ta_size)
    link = load_links(packed, 0, 1, 2, 3)
    link_first = chosen_matrix(last, link[3], link[2])
    forward_first = jnp.where(last, 1 - odd_t, core) == 1
    clov = [load_matrix(clover, 0), load_matrix(clover, 1)]
    for at in range(0, columns, ROWS):
        rows = pl.ds(at, ROWS)
        field = load_field(src, rows, 4)
        hop = [[None] * 4 for _ in range(3)]
        for direction in range(2):
            minus = half(field, direction, False)
            ahead = [
                [tuple(shift_sites(v, direction, True) for v in rounded(minus[c][s])) for s in range(2)]
                for c in range(3)
            ]
            plus = half(field, direction, True)
            for a in range(3):
                w = [color_row(link[direction], ahead, a, s, False) for s in range(2)]
                g = [
                    tuple(
                        shift_sites(v, direction, False)
                        for v in rounded(color_row(link[direction], plus, a, s, True))
                    )
                    for s in range(2)
                ]
                upper = [add(w[s], g[s]) for s in range(2)]
                add_to(hop, a, upper + spin_dagger(direction, [sub(g[s], w[s]) for s in range(2)]))
        add_swapped(hop, link[2], load_field(cores.at[1 - core], rows, 2), core == 0, turned_z)
        add_swapped(hop, link_first, load_field(first, rows, 2), forward_first, functools.partial(turned_either, last))
        add_swapped(hop, link[3], load_field(second, rows, 2), odd_t == 1, turned_t, ahead_sign, behind_sign)
        for a in range(3):
            for s in range(4):
                own = add(field[a][s], color_row(clov[s // 2], field, a, s, False))
                for q in range(2):
                    out[q, a, s, rows, :] = own[q] - KAPPA * hop[a][s][q]


def finish_kernel(ta_size, local, packed, third, vectors, result, partial):
    columns = local.shape[3]
    core, odd_t, last, _, _ = place_on_mesh(ta_size)
    link = chosen_matrix(last, *load_links(packed, 2, 3))
    forward = jnp.where(last, core, 1 - odd_t) == 1
    turn = functools.partial(turned_either, jnp.logical_not(last))
    for at in range(0, columns, ROWS):
        rows = pl.ds(at, ROWS)
        hop = [[None] * 4 for _ in range(3)]
        add_swapped(hop, link, load_field(third, rows, 2), forward, turn)
        for a in range(3):
            for s in range(4):
                for q in range(2):
                    value = local[q, a, s, rows, :] - KAPPA * hop[a][s][q]
                    result[q, a, s, rows, :] = value.astype(BF16)
    total = None
    contract = (((1,), (1,)), ((), ()))
    for c in range(3):
        left_re = vectors[0, c]
        left_im = vectors[1, c]
        for q in range(2):
            right = result[q, c].reshape(4 * columns, result.shape[4])
            left = [left_re, -left_im] if q == 0 else [left_im, left_re]
            term = lax.dot_general(jnp.concatenate(left, axis=0), right, contract, preferred_element_type=F32)
            total = term if total is None else total + term
    partial[...] = total.reshape(partial.shape)


def copy_kernel(src, out):
    out[...] = src[...]


def call(body, outs, operands, flops, in_specs=None, scratch_shapes=()):
    vmem = pl.BlockSpec(memory_space=pltpu.VMEM)
    moved = sum(x.size * x.dtype.itemsize for x in list(outs) + list(operands))
    return pl.pallas_call(
        body,
        out_shape=outs,
        in_specs=in_specs or [vmem] * len(operands),
        out_specs=[vmem] * len(outs),
        scratch_shapes=scratch_shapes,
        compiler_params=pltpu.CompilerParams(vmem_limit_bytes=32 * 2**20),
        cost_estimate=pl.CostEstimate(flops=flops, bytes_accessed=moved, transcendentals=0),
    )(*operands)


def gathered_sum(x, groups):
    both = lax.all_gather(x, "sa", axis_index_groups=groups).astype(F32)
    return lax.reduce_precision(both[0] + both[1], 8, 7).astype(BF16)


def sum_over_blocks(partial, size):
    plane = 8
    planes = size // plane
    cores = [[i, i + 1] for i in range(0, size, 2)]
    starts = range(0, size, plane)
    even = [[z + 4 * p + c, z + 4 * p + 2 + c] for z in starts for p in range(2) for c in range(2)]
    odd = [[z + 2 + c, z + 4 + c] for z in starts for c in range(2)]
    odd += [[z + c, z + 6 + c] for z in starts for c in range(2)]
    s = gathered_sum(partial, cores)
    row = [[z + 2 * x + c for x in range(4)] for z in starts for c in range(2)]
    four = lax.all_to_all(jnp.broadcast_to(s[None], (4,) + s.shape), "sa", 0, 0, axis_index_groups=row).astype(F32)
    s = lax.reduce_precision((four[0] + four[1]) + (four[2] + four[3]), 8, 7).astype(BF16)
    pairs = []
    for i in range(size):
        z, r = divmod(i, plane)
        step = 1 if i % 2 else planes - 1
        pairs.append((i, ((z + step) % planes) * plane + r))
    other = lax.all_gather(lax.ppermute(s, "sa", pairs), "sa", axis_index_groups=cores)
    z = lax.axis_index("sa") // plane
    own, nxt, last = s.astype(F32), other[0].astype(F32), other[1].astype(F32)
    first = jnp.where(z == 0, own, jnp.where(z == 1, last, nxt))
    second = jnp.where(z == 0, nxt, jnp.where(z == 1, own, last))
    third = jnp.where(z == 0, last, jnp.where(z == 1, nxt, own))
    return first + second + third


def shards(source_field, gauge_links, clover, eigenvectors):
    sites = source_field.shape[-1]
    columns = source_field.shape[3]
    ta, sa = lax.axis_size("ta"), lax.axis_size("sa")
    src = source_field.reshape(2, 3, 4, columns, sites)
    links = gauge_links.reshape(2, 4, 3, 3, sites).transpose(0, 2, 3, 1, 4)
    clov = clover.reshape(2, 2, 3, 3, sites).transpose(0, 2, 3, 1, 4)
    vectors = eigenvectors.reshape(2, 3, eigenvectors.shape[2], sites)
    half_shape = jax.ShapeDtypeStruct((2, 3, 2, columns, sites), BF16)
    points = columns * sites

    packed = jnp.concatenate([src.reshape(-1, sites), links.reshape(-1, sites)])
    to_core, to_first, to_second, to_third = call(
        functools.partial(edge_kernel, ta),
        [half_shape] * 4,
        (packed,),
        500 * points,
    )

    def place(t, z):
        return (t % ta) * sa + z % sa

    def along_z(slabs):
        return [(place(t, z), place(t, z + (1 if z % 2 else -1))) for t in slabs for z in range(sa)]

    def along_t(slabs, parity):
        return [(place(t, z), place(t + (1 if t % 2 == parity else -1), z)) for t in slabs for z in range(sa)]

    most, rest = range(ta - 2), range(ta - 2, ta)
    first = lax.ppermute(to_first, ("ta", "sa"), along_z(most) + along_t(rest, 0))
    second = lax.ppermute(to_second, ("ta", "sa"), along_t(range(ta), 1))
    third = lax.ppermute(to_third, ("ta", "sa"), along_t(most, 0) + along_z(rest))
    cores = lax.all_gather(to_core, "sa", axis_index_groups=[[i, i + 1] for i in range(0, sa, 2)])
    (local,) = call(
        functools.partial(local_kernel, ta),
        [jax.ShapeDtypeStruct((2, 3, 4, columns, sites), F32)],
        (packed, clov, cores, first, second),
        2500 * points,
    )
    result, partial = call(
        functools.partial(finish_kernel, ta),
        [
            jax.ShapeDtypeStruct((2, 3, 4, columns, sites), BF16),
            jax.ShapeDtypeStruct((2, vectors.shape[2], 4 * columns), F32),
        ],
        (local, packed, third, vectors),
        500 * points,
    )
    perambulator = sum_over_blocks(partial, sa)
    (result,) = call(copy_kernel, [jax.ShapeDtypeStruct(result.shape, BF16)], (result,), 2000 * points)
    return result.reshape(source_field.shape), perambulator[:, None]


def solution(mesh):
    in_specs = (
        P(None, None, None, None, "ta", "sa", None),
        P(None, None, None, None, "ta", "sa", None),
        P(None, None, None, None, "ta", "sa", None),
        P(None, None, None, "ta", "sa", None),
    )
    out_specs = (P(None, None, None, None, "ta", "sa", None), P(None, "ta", None, None))
    return jax.shard_map(shards, mesh=mesh, in_specs=in_specs, out_specs=out_specs, check_vma=False)
```

```python
import functools

import jax
import jax.numpy as jnp
from jax import lax
from jax.experimental import pallas as pl
from jax.experimental.pallas import tpu as pltpu
from jax.sharding import PartitionSpec as P

KAPPA = 0.125
ROWS = 16
LINK_ROWS = 72
F32 = jnp.float32
BF16 = jnp.bfloat16


def add(a, b):
    return (a[0] + b[0], a[1] + b[1])


def sub(a, b):
    return (a[0] - b[0], a[1] - b[1])


def neg(a):
    return (-a[0], -a[1])


def times_i(a):
    return (-a[1], a[0])


def spin(direction, w):
    if direction == 0:
        return [neg(times_i(w[1])), neg(times_i(w[0]))]
    if direction == 1:
        return [neg(w[1]), w[0]]
    if direction == 2:
        return [neg(times_i(w[0])), times_i(w[1])]
    return [w[0], w[1]]


def spin_dagger(direction, w):
    if direction == 0:
        return [times_i(w[1]), times_i(w[0])]
    if direction == 1:
        return [w[1], neg(w[0])]
    if direction == 2:
        return [times_i(w[0]), neg(times_i(w[1]))]
    return [w[0], w[1]]


def rounded(a):
    return (a[0].astype(BF16).astype(F32), a[1].astype(BF16).astype(F32))


def load_field(ref, rows, spins):
    return [
        [(ref[0, c, s, rows, :].astype(F32), ref[1, c, s, rows, :].astype(F32)) for s in range(spins)]
        for c in range(3)
    ]


class Field:
    def __init__(self, packed):
        self.packed, self.shape = packed, (2, 3, 4, (packed.shape[0] - LINK_ROWS) // 24, packed.shape[1])

    def __getitem__(self, at):
        q, c, s, rows, _ = at
        return self.packed[pl.ds(((q * 3 + c) * 4 + s) * self.shape[3] + rows.start, rows.size), :]


def load_links(packed, *directions):
    block = packed[pl.ds(packed.shape[0] - LINK_ROWS, LINK_ROWS), :].astype(F32)

    def row(q, a, b, direction):
        at = ((q * 3 + a) * 3 + b) * 4 + direction
        return block[at : at + 1, :]

    return [
        [[(row(0, a, b, direction), row(1, a, b, direction)) for b in range(3)] for a in range(3)]
        for direction in directions
    ]


def load_matrix(ref, which):
    tiles = [[[ref[q, a, b, :, :].astype(F32) for b in range(3)] for a in range(3)] for q in range(2)]
    return [
        [(tiles[0][a][b][which : which + 1, :], tiles[1][a][b][which : which + 1, :]) for b in range(3)]
        for a in range(3)
    ]


def color_row(matrix, part, a, s, dagger):
    re = im = None
    for b in range(3):
        x_re, x_im = part[b][s]
        if dagger:
            m_re, m_im = matrix[b][a]
            terms = (m_re * x_re + m_im * x_im, m_re * x_im - m_im * x_re)
        else:
            m_re, m_im = matrix[a][b]
            terms = (m_re * x_re - m_im * x_im, m_re * x_im + m_im * x_re)
        re = terms[0] if re is None else re + terms[0]
        im = terms[1] if im is None else im + terms[1]
    return (re, im)


def half(field, direction, plus):
    out = []
    for c in range(3):
        turned = spin(direction, [field[c][2], field[c][3]])
        out.append([(add if plus else sub)(field[c][s], turned[s]) for s in range(2)])
    return out


def late_slabs(me, ta_size):
    return me >= ta_size - 4, (me == ta_size - 3) | (me == ta_size - 2)


def edge_kernel(ta_size, packed, to_core, to_first, to_second, to_third):
    src = Field(packed)
    columns = src.shape[3]
    link_z, link_t = load_links(packed, 2, 3)
    me = lax.axis_index("ta")
    even_z = lax.axis_index("sa") % 2 == 0
    even_t = me % 2 == 0
    late, middle = late_slabs(me, ta_size)
    for at in range(0, columns, ROWS):
        rows = pl.ds(at, ROWS)
        field = load_field(src, rows, 4)
        minus_z, minus_t = half(field, 2, False), half(field, 3, False)
        plus_z, plus_t = half(field, 2, True), half(field, 3, True)
        for a in range(3):
            for s in range(2):
                back_z = color_row(link_z, plus_z, a, s, True)
                back_t = color_row(link_t, plus_t, a, s, True)
                for q in range(2):
                    to_core[q, a, s, rows, :] = jnp.where(even_z, back_z[q], minus_z[a][s][q]).astype(BF16)
                    chip = jnp.where(even_z, minus_z[a][s][q], back_z[q])
                    even = jnp.where(even_t, back_t[q], minus_t[a][s][q])
                    odd = jnp.where(even_t, minus_t[a][s][q], back_t[q])
                    to_first[q, a, s, rows, :] = jnp.where(late, even, chip).astype(BF16)
                    to_second[q, a, s, rows, :] = jnp.where(middle, chip, odd).astype(BF16)
                    third = jnp.where(middle, odd, jnp.where(late, chip, even))
                    to_third[q, a, s, rows, :] = third.astype(BF16)


def shift_sites(x, direction, ahead):
    lane = lax.broadcasted_iota(jnp.int32, x.shape, 1)
    if direction == 1:
        return pltpu.roll(x, 120 if ahead else 8, 1)
    if ahead:
        return jnp.where(lane % 8 == 7, pltpu.roll(x, 7, 1), pltpu.roll(x, 127, 1))
    return jnp.where(lane % 8 == 0, pltpu.roll(x, 121, 1), pltpu.roll(x, 1, 1))


def add_to(hop, a, values):
    for s, v in enumerate(values):
        hop[a][s] = v if hop[a][s] is None else add(hop[a][s], v)


def place_on_mesh(ta_size):
    me, core = lax.axis_index("ta"), lax.axis_index("sa") % 2
    ahead_sign = jnp.where(me == ta_size - 1, -1.0, 1.0).astype(F32)
    behind_sign = jnp.where(me == 0, -1.0, 1.0).astype(F32)
    return core, me % 2, *late_slabs(me, ta_size), ahead_sign, behind_sign


def chosen_matrix(first, a, b):
    return [[tuple(jnp.where(first, p, q) for p, q in zip(v, w)) for v, w in zip(x, y)] for x, y in zip(a, b)]


def add_swapped(hop, link, part, forward, turn, forward_sign=None, backward_sign=None):
    for a in range(3):
        upper, signed = [], []
        for s in range(2):
            w, g = color_row(link, part, a, s, False), part[a][s]
            if forward_sign is not None:
                w = (w[0] * forward_sign, w[1] * forward_sign)
                g = (g[0] * backward_sign, g[1] * backward_sign)
            upper.append(tuple(jnp.where(forward, p, q) for p, q in zip(w, g)))
            signed.append(tuple(jnp.where(forward, -p, q) for p, q in zip(w, g)))
        add_to(hop, a, upper + turn(signed))


def turned_z(w):
    return spin_dagger(2, w)


def turned_t(w):
    return spin_dagger(3, w)


def turned_either(along_t, w):
    return [
        tuple(jnp.where(along_t, p, q) for p, q in zip(v, u)) for v, u in zip(turned_t(w), turned_z(w))
    ]


def local_kernel(ta_size, packed, clover, cores, first, second, out):
    src = Field(packed)
    columns = src.shape[3]
    core, odd_t, late, middle, ahead_sign, behind_sign = place_on_mesh(ta_size)
    link = load_links(packed, 0, 1, 2, 3)
    link_first = chosen_matrix(late, link[3], link[2])
    link_second = chosen_matrix(middle, link[2], link[3])
    forward_first = jnp.where(late, 1 - odd_t, core) == 1
    forward_second = jnp.where(middle, core, odd_t) == 1
    turn_first = functools.partial(turned_either, late)
    turn_second = functools.partial(turned_either, jnp.logical_not(middle))
    clov = [load_matrix(clover, 0), load_matrix(clover, 1)]
    for at in range(0, columns, ROWS):
        rows = pl.ds(at, ROWS)
        field = load_field(src, rows, 4)
        hop = [[None] * 4 for _ in range(3)]
        for direction in range(2):
            minus = half(field, direction, False)
            ahead = [
                [tuple(shift_sites(v, direction, True) for v in rounded(minus[c][s])) for s in range(2)]
                for c in range(3)
            ]
            plus = half(field, direction, True)
            for a in range(3):
                w = [color_row(link[direction], ahead, a, s, False) for s in range(2)]
                g = [
                    tuple(
                        shift_sites(v, direction, False)
                        for v in rounded(color_row(link[direction], plus, a, s, True))
                    )
                    for s in range(2)
                ]
                upper = [add(w[s], g[s]) for s in range(2)]
                add_to(hop, a, upper + spin_dagger(direction, [sub(g[s], w[s]) for s in range(2)]))
        add_swapped(hop, link[2], load_field(cores.at[1 - core], rows, 2), core == 0, turned_z)
        add_swapped(hop, link_first, load_field(first, rows, 2), forward_first, turn_first)
        part = load_field(second, rows, 2)
        add_swapped(hop, link_second, part, forward_second, turn_second, ahead_sign, behind_sign)
        for a in range(3):
            for s in range(4):
                own = add(field[a][s], color_row(clov[s // 2], field, a, s, False))
                for q in range(2):
                    out[q, a, s, rows, :] = own[q] - KAPPA * hop[a][s][q]


def finish_kernel(ta_size, local, packed, third, vectors, result, partial):
    columns = local.shape[3]
    core, odd_t, late, middle, _, _ = place_on_mesh(ta_size)
    along_z = late & jnp.logical_not(middle)
    link = chosen_matrix(along_z, *load_links(packed, 2, 3))
    forward = jnp.where(middle, odd_t, jnp.where(late, core, 1 - odd_t)) == 1
    turn = functools.partial(turned_either, jnp.logical_not(along_z))
    for at in range(0, columns, ROWS):
        rows = pl.ds(at, ROWS)
        hop = [[None] * 4 for _ in range(3)]
        add_swapped(hop, link, load_field(third, rows, 2), forward, turn)
        for a in range(3):
            for s in range(4):
                for q in range(2):
                    value = local[q, a, s, rows, :] - KAPPA * hop[a][s][q]
                    result[q, a, s, rows, :] = value.astype(BF16)
    total = None
    contract = (((1,), (1,)), ((), ()))
    for c in range(3):
        left_re = vectors[0, c]
        left_im = vectors[1, c]
        for q in range(2):
            right = result[q, c].reshape(4 * columns, result.shape[4])
            left = [left_re, -left_im] if q == 0 else [left_im, left_re]
            term = lax.dot_general(jnp.concatenate(left, axis=0), right, contract, preferred_element_type=F32)
            total = term if total is None else total + term
    partial[...] = total.reshape(partial.shape)


def copy_kernel(src, out):
    out[...] = src[...]


def call(body, outs, operands, flops, in_specs=None, scratch_shapes=()):
    vmem = pl.BlockSpec(memory_space=pltpu.VMEM)
    moved = sum(x.size * x.dtype.itemsize for x in list(outs) + list(operands))
    return pl.pallas_call(
        body,
        out_shape=outs,
        in_specs=in_specs or [vmem] * len(operands),
        out_specs=[vmem] * len(outs),
        scratch_shapes=scratch_shapes,
        compiler_params=pltpu.CompilerParams(vmem_limit_bytes=32 * 2**20),
        cost_estimate=pl.CostEstimate(flops=flops, bytes_accessed=moved, transcendentals=0),
    )(*operands)


def gathered_sum(x, groups):
    both = lax.all_gather(x, "sa", axis_index_groups=groups).astype(F32)
    return lax.reduce_precision(both[0] + both[1], 8, 7).astype(BF16)


def sum_over_blocks(partial, result, size):
    plane = 8
    planes = size // plane
    cores = [[i, i + 1] for i in range(0, size, 2)]
    starts = range(0, size, plane)
    even = [[z + 4 * p + c, z + 4 * p + 2 + c] for z in starts for p in range(2) for c in range(2)]
    odd = [[z + 2 + c, z + 4 + c] for z in starts for c in range(2)]
    odd += [[z + c, z + 6 + c] for z in starts for c in range(2)]
    row = [[z + 2 * x + c for x in range(4)] for z in starts for c in range(2)]
    s = gathered_sum(partial, cores)
    pairs = []
    for i in range(size):
        z, r = divmod(i, plane)
        step = 1 if i % 2 else planes - 1
        pairs.append((i, ((z + step) % planes) * plane + r))
    other = lax.ppermute(s, "sa", pairs)
    (result,) = call(copy_kernel, [jax.ShapeDtypeStruct(result.shape, BF16)], (result,), result.size)
    other, result = lax.optimization_barrier((other, result))
    other = lax.all_gather(other, "sa", axis_index_groups=cores)
    z = lax.axis_index("sa") // plane
    own, nxt, last = s.astype(F32), other[0].astype(F32), other[1].astype(F32)
    first = jnp.where(z == 0, own, jnp.where(z == 1, last, nxt))
    second = jnp.where(z == 0, nxt, jnp.where(z == 1, own, last))
    third = jnp.where(z == 0, last, jnp.where(z == 1, nxt, own))
    s = lax.reduce_precision(first + second + third, 8, 7).astype(BF16)
    four = lax.all_to_all(jnp.broadcast_to(s[None], (4,) + s.shape), "sa", 0, 0, axis_index_groups=row).astype(F32)
    return (four[0] + four[1]) + (four[2] + four[3]), result


def shards(source_field, gauge_links, clover, eigenvectors):
    sites = source_field.shape[-1]
    columns = source_field.shape[3]
    ta, sa = lax.axis_size("ta"), lax.axis_size("sa")
    src = source_field.reshape(2, 3, 4, columns, sites)
    links = gauge_links.reshape(2, 4, 3, 3, sites).transpose(0, 2, 3, 1, 4)
    clov = clover.reshape(2, 2, 3, 3, sites).transpose(0, 2, 3, 1, 4)
    vectors = eigenvectors.reshape(2, 3, eigenvectors.shape[2], sites)
    half_shape = jax.ShapeDtypeStruct((2, 3, 2, columns, sites), BF16)
    points = columns * sites

    packed = jnp.concatenate([src.reshape(-1, sites), links.reshape(-1, sites)])
    to_core, to_first, to_second, to_third = call(
        functools.partial(edge_kernel, ta),
        [half_shape] * 4,
        (packed,),
        500 * points,
    )

    def place(t, z):
        return (t % ta) * sa + z % sa

    def along_z(slabs):
        return [(place(t, z), place(t, z + (1 if z % 2 else -1))) for t in slabs for z in range(sa)]

    def along_t(slabs, parity):
        return [(place(t, z), place(t + (1 if t % 2 == parity else -1), z)) for t in slabs for z in range(sa)]

    early, late, middle, ends = range(ta - 4), range(ta - 4, ta), (ta - 3, ta - 2), (ta - 4, ta - 1)
    others = [t for t in range(ta) if t not in middle]
    first = lax.ppermute(to_first, ("ta", "sa"), along_z(early) + along_t(late, 0))
    second = lax.ppermute(to_second, ("ta", "sa"), along_t(others, 1) + along_z(middle))
    third = lax.ppermute(to_third, ("ta", "sa"), along_t(early, 0) + along_z(ends) + along_t(middle, 1))
    cores = lax.all_gather(to_core, "sa", axis_index_groups=[[i, i + 1] for i in range(0, sa, 2)])
    (local,) = call(
        functools.partial(local_kernel, ta),
        [jax.ShapeDtypeStruct((2, 3, 4, columns, sites), F32)],
        (packed, clov, cores, first, second),
        2500 * points,
    )
    result, partial = call(
        functools.partial(finish_kernel, ta),
        [
            jax.ShapeDtypeStruct((2, 3, 4, columns, sites), BF16),
            jax.ShapeDtypeStruct((2, vectors.shape[2], 4 * columns), F32),
        ],
        (local, packed, third, vectors),
        500 * points,
    )
    perambulator, result = sum_over_blocks(partial, result, sa)
    return result.reshape(source_field.shape), perambulator[:, None]


def solution(mesh):
    in_specs = (
        P(None, None, None, None, "ta", "sa", None),
        P(None, None, None, None, "ta", "sa", None),
        P(None, None, None, None, "ta", "sa", None),
        P(None, None, None, "ta", "sa", None),
    )
    out_specs = (P(None, None, None, None, "ta", "sa", None), P(None, "ta", None, None))
    return jax.shard_map(shards, mesh=mesh, in_specs=in_specs, out_specs=out_specs, check_vma=False)
```

```python
import functools

import jax
import jax.numpy as jnp
from jax import lax
from jax.experimental import pallas as pl
from jax.experimental.pallas import tpu as pltpu
from jax.sharding import PartitionSpec as P

KAPPA = 0.125
ROWS = 16
LINK_ROWS = 72
F32 = jnp.float32
BF16 = jnp.bfloat16


def add(a, b):
    return (a[0] + b[0], a[1] + b[1])


def sub(a, b):
    return (a[0] - b[0], a[1] - b[1])


def neg(a):
    return (-a[0], -a[1])


def times_i(a):
    return (-a[1], a[0])


def spin(direction, w):
    if direction == 0:
        return [neg(times_i(w[1])), neg(times_i(w[0]))]
    if direction == 1:
        return [neg(w[1]), w[0]]
    if direction == 2:
        return [neg(times_i(w[0])), times_i(w[1])]
    return [w[0], w[1]]


def spin_dagger(direction, w):
    if direction == 0:
        return [times_i(w[1]), times_i(w[0])]
    if direction == 1:
        return [w[1], neg(w[0])]
    if direction == 2:
        return [times_i(w[0]), neg(times_i(w[1]))]
    return [w[0], w[1]]


def rounded(a):
    return (a[0].astype(BF16).astype(F32), a[1].astype(BF16).astype(F32))


def load_field(ref, rows, spins):
    return [
        [(ref[0, c, s, rows, :].astype(F32), ref[1, c, s, rows, :].astype(F32)) for s in range(spins)]
        for c in range(3)
    ]


class Field:
    def __init__(self, packed):
        self.packed, self.shape = packed, (2, 3, 4, (packed.shape[0] - LINK_ROWS) // 24, packed.shape[1])

    def __getitem__(self, at):
        q, c, s, rows, _ = at
        return self.packed[pl.ds(((q * 3 + c) * 4 + s) * self.shape[3] + rows.start, rows.size), :]


def load_links(packed, *directions):
    block = packed[pl.ds(packed.shape[0] - LINK_ROWS, LINK_ROWS), :].astype(F32)

    def row(q, a, b, direction):
        at = ((q * 3 + a) * 3 + b) * 4 + direction
        return block[at : at + 1, :]

    return [
        [[(row(0, a, b, direction), row(1, a, b, direction)) for b in range(3)] for a in range(3)]
        for direction in directions
    ]


def load_matrix(ref, which):
    tiles = [[[ref[q, a, b, :, :].astype(F32) for b in range(3)] for a in range(3)] for q in range(2)]
    return [
        [(tiles[0][a][b][which : which + 1, :], tiles[1][a][b][which : which + 1, :]) for b in range(3)]
        for a in range(3)
    ]


def color_row(matrix, part, a, s, dagger):
    re = im = None
    for b in range(3):
        x_re, x_im = part[b][s]
        if dagger:
            m_re, m_im = matrix[b][a]
            terms = (m_re * x_re + m_im * x_im, m_re * x_im - m_im * x_re)
        else:
            m_re, m_im = matrix[a][b]
            terms = (m_re * x_re - m_im * x_im, m_re * x_im + m_im * x_re)
        re = terms[0] if re is None else re + terms[0]
        im = terms[1] if im is None else im + terms[1]
    return (re, im)


def half(field, direction, plus):
    out = []
    for c in range(3):
        turned = spin(direction, [field[c][2], field[c][3]])
        out.append([(add if plus else sub)(field[c][s], turned[s]) for s in range(2)])
    return out


def knot(ta_size, sa_size):
    me, z = lax.axis_index("ta"), lax.axis_index("sa")
    far = (z == 2 * sa_size // 3 - 1) | (z == 2 * sa_size // 3)
    return far & (me >= ta_size - 2), far & (me == ta_size - 1)


def edge_kernel(sizes, packed, to_core, to_zeroth, to_first, to_second, to_third):
    src = Field(packed)
    columns = src.shape[3]
    link_z, link_t = load_links(packed, 2, 3)
    me = lax.axis_index("ta")
    even_z = lax.axis_index("sa") % 2 == 0
    even_t = me % 2 == 0
    late, last = knot(*sizes)
    for at in range(0, columns, ROWS):
        rows = pl.ds(at, ROWS)
        field = load_field(src, rows, 4)
        minus_z, minus_t = half(field, 2, False), half(field, 3, False)
        plus_z, plus_t = half(field, 2, True), half(field, 3, True)
        for a in range(3):
            for s in range(2):
                back_z = color_row(link_z, plus_z, a, s, True)
                back_t = color_row(link_t, plus_t, a, s, True)
                for q in range(2):
                    to_core[q, a, s, rows, :] = jnp.where(even_z, back_z[q], minus_z[a][s][q]).astype(BF16)
                    chip = jnp.where(even_z, minus_z[a][s][q], back_z[q])
                    even = jnp.where(even_t, back_t[q], minus_t[a][s][q])
                    odd = jnp.where(even_t, minus_t[a][s][q], back_t[q])
                    to_zeroth[q, a, s, rows, :] = jnp.where(late, even, odd).astype(BF16)
                    to_first[q, a, s, rows, :] = chip.astype(BF16)
                    to_second[q, a, s, rows, :] = odd.astype(BF16)
                    to_third[q, a, s, rows, :] = jnp.where(last, chip, even).astype(BF16)


def shift_sites(x, direction, ahead):
    lane = lax.broadcasted_iota(jnp.int32, x.shape, 1)
    if direction == 1:
        return pltpu.roll(x, 120 if ahead else 8, 1)
    if ahead:
        return jnp.where(lane % 8 == 7, pltpu.roll(x, 7, 1), pltpu.roll(x, 127, 1))
    return jnp.where(lane % 8 == 0, pltpu.roll(x, 121, 1), pltpu.roll(x, 1, 1))


def add_to(hop, a, values):
    for s, v in enumerate(values):
        hop[a][s] = v if hop[a][s] is None else add(hop[a][s], v)


def place_on_mesh(ta_size):
    me, core = lax.axis_index("ta"), lax.axis_index("sa") % 2
    ahead_sign = jnp.where(me == ta_size - 1, -1.0, 1.0).astype(F32)
    behind_sign = jnp.where(me == 0, -1.0, 1.0).astype(F32)
    return core, me % 2, ahead_sign, behind_sign


def chosen_matrix(first, a, b):
    return [[tuple(jnp.where(first, p, q) for p, q in zip(v, w)) for v, w in zip(x, y)] for x, y in zip(a, b)]


def add_swapped(hop, link, part, forward, turn, forward_sign=None, backward_sign=None):
    for a in range(3):
        upper, signed = [], []
        for s in range(2):
            w, g = color_row(link, part, a, s, False), part[a][s]
            if forward_sign is not None:
                w = (w[0] * forward_sign, w[1] * forward_sign)
                g = (g[0] * backward_sign, g[1] * backward_sign)
            upper.append(tuple(jnp.where(forward, p, q) for p, q in zip(w, g)))
            signed.append(tuple(jnp.where(forward, -p, q) for p, q in zip(w, g)))
        add_to(hop, a, upper + turn(signed))


def turned_z(w):
    return spin_dagger(2, w)


def turned_t(w):
    return spin_dagger(3, w)


def turned_either(along_t, w):
    return [
        tuple(jnp.where(along_t, p, q) for p, q in zip(v, u)) for v, u in zip(turned_t(w), turned_z(w))
    ]


def local_kernel(sizes, packed, clover, cores, zeroth, first, second, out):
    src = Field(packed)
    columns = src.shape[3]
    core, odd_t, ahead_sign, behind_sign = place_on_mesh(sizes[0])
    late, _ = knot(*sizes)
    link = load_links(packed, 0, 1, 2, 3)
    forward_zeroth = jnp.where(late, 1 - odd_t, odd_t) == 1
    clov = [load_matrix(clover, 0), load_matrix(clover, 1)]
    for at in range(0, columns, ROWS):
        rows = pl.ds(at, ROWS)
        field = load_field(src, rows, 4)
        hop = [[None] * 4 for _ in range(3)]
        for direction in range(2):
            minus = half(field, direction, False)
            ahead = [
                [tuple(shift_sites(v, direction, True) for v in rounded(minus[c][s])) for s in range(2)]
                for c in range(3)
            ]
            plus = half(field, direction, True)
            for a in range(3):
                w = [color_row(link[direction], ahead, a, s, False) for s in range(2)]
                g = [
                    tuple(
                        shift_sites(v, direction, False)
                        for v in rounded(color_row(link[direction], plus, a, s, True))
                    )
                    for s in range(2)
                ]
                upper = [add(w[s], g[s]) for s in range(2)]
                add_to(hop, a, upper + spin_dagger(direction, [sub(g[s], w[s]) for s in range(2)]))
        add_swapped(hop, link[2], load_field(cores.at[1 - core], rows, 2), core == 0, turned_z)
        add_swapped(hop, link[2], load_field(first, rows, 2), core == 1, turned_z)
        add_swapped(hop, link[3], load_field(second, rows, 2), odd_t == 1, turned_t, ahead_sign, behind_sign)
        add_swapped(hop, link[3], load_field(zeroth, rows, 2), forward_zeroth, turned_t, ahead_sign, behind_sign)
        for a in range(3):
            for s in range(4):
                own = add(field[a][s], color_row(clov[s // 2], field, a, s, False))
                for q in range(2):
                    out[q, a, s, rows, :] = own[q] - KAPPA * hop[a][s][q]


def finish_kernel(sizes, local, packed, third, vectors, result, partial):
    columns = local.shape[3]
    core, odd_t, _, _ = place_on_mesh(sizes[0])
    _, last = knot(*sizes)
    link = chosen_matrix(last, *load_links(packed, 2, 3))
    forward = jnp.where(last, core, 1 - odd_t) == 1
    turn = functools.partial(turned_either, jnp.logical_not(last))
    for at in range(0, columns, ROWS):
        rows = pl.ds(at, ROWS)
        hop = [[None] * 4 for _ in range(3)]
        add_swapped(hop, link, load_field(third, rows, 2), forward, turn)
        for a in range(3):
            for s in range(4):
                for q in range(2):
                    value = local[q, a, s, rows, :] - KAPPA * hop[a][s][q]
                    result[q, a, s, rows, :] = value.astype(BF16)
    total = None
    contract = (((1,), (1,)), ((), ()))
    for c in range(3):
        left_re = vectors[0, c]
        left_im = vectors[1, c]
        for q in range(2):
            right = result[q, c].reshape(4 * columns, result.shape[4])
            left = [left_re, -left_im] if q == 0 else [left_im, left_re]
            term = lax.dot_general(jnp.concatenate(left, axis=0), right, contract, preferred_element_type=F32)
            total = term if total is None else total + term
    partial[...] = total.reshape(partial.shape)


def copy_kernel(src, out):
    out[...] = src[...]


def call(body, outs, operands, flops, in_specs=None, scratch_shapes=()):
    vmem = pl.BlockSpec(memory_space=pltpu.VMEM)
    moved = sum(x.size * x.dtype.itemsize for x in list(outs) + list(operands))
    return pl.pallas_call(
        body,
        out_shape=outs,
        in_specs=in_specs or [vmem] * len(operands),
        out_specs=[vmem] * len(outs),
        scratch_shapes=scratch_shapes,
        compiler_params=pltpu.CompilerParams(vmem_limit_bytes=32 * 2**20),
        cost_estimate=pl.CostEstimate(flops=flops, bytes_accessed=moved, transcendentals=0),
    )(*operands)


def gathered_sum(x, groups):
    both = lax.all_gather(x, "sa", axis_index_groups=groups).astype(F32)
    return lax.reduce_precision(both[0] + both[1], 8, 7).astype(BF16)


def sum_over_blocks(partial, result, size):
    plane = 8
    planes = size // plane
    cores = [[i, i + 1] for i in range(0, size, 2)]
    starts = range(0, size, plane)
    even = [[z + 4 * p + c, z + 4 * p + 2 + c] for z in starts for p in range(2) for c in range(2)]
    odd = [[z + 2 + c, z + 4 + c] for z in starts for c in range(2)]
    odd += [[z + c, z + 6 + c] for z in starts for c in range(2)]
    row = [[z + 2 * x + c for x in range(4)] for z in starts for c in range(2)]
    s = gathered_sum(partial, cores)
    pairs = []
    for i in range(size):
        z, r = divmod(i, plane)
        step = 1 if i % 2 else planes - 1
        pairs.append((i, ((z + step) % planes) * plane + r))
    other = lax.ppermute(s, "sa", pairs)
    (result,) = call(copy_kernel, [jax.ShapeDtypeStruct(result.shape, BF16)], (result,), result.size)
    other, result = lax.optimization_barrier((other, result))
    other = lax.all_gather(other, "sa", axis_index_groups=cores)
    z = lax.axis_index("sa") // plane
    own, nxt, last = s.astype(F32), other[0].astype(F32), other[1].astype(F32)
    first = jnp.where(z == 0, own, jnp.where(z == 1, last, nxt))
    second = jnp.where(z == 0, nxt, jnp.where(z == 1, own, last))
    third = jnp.where(z == 0, last, jnp.where(z == 1, nxt, own))
    s = lax.reduce_precision(first + second + third, 8, 7).astype(BF16)
    four = lax.all_to_all(jnp.broadcast_to(s[None], (4,) + s.shape), "sa", 0, 0, axis_index_groups=row).astype(F32)
    return (four[0] + four[1]) + (four[2] + four[3]), result


def shards(source_field, gauge_links, clover, eigenvectors):
    sites = source_field.shape[-1]
    columns = source_field.shape[3]
    ta, sa = lax.axis_size("ta"), lax.axis_size("sa")
    src = source_field.reshape(2, 3, 4, columns, sites)
    links = gauge_links.reshape(2, 4, 3, 3, sites).transpose(0, 2, 3, 1, 4)
    clov = clover.reshape(2, 2, 3, 3, sites).transpose(0, 2, 3, 1, 4)
    vectors = eigenvectors.reshape(2, 3, eigenvectors.shape[2], sites)
    half_shape = jax.ShapeDtypeStruct((2, 3, 2, columns, sites), BF16)
    points = columns * sites

    packed = jnp.concatenate([src.reshape(-1, sites), links.reshape(-1, sites)])
    to_core, to_zeroth, to_first, to_second, to_third = call(
        functools.partial(edge_kernel, (ta, sa)),
        [half_shape] * 5,
        (packed,),
        500 * points,
    )

    def place(t, z):
        return (t % ta) * sa + z % sa

    def along_z(slabs, blocks):
        return [(place(t, z), place(t, z + (1 if z % 2 else -1))) for t in slabs for z in blocks]

    def along_t(slabs, parity, blocks):
        return [(place(t, z), place(t + (1 if t % 2 == parity else -1), z)) for t in slabs for z in blocks]

    slabs, late, last = range(ta), (ta - 2, ta - 1), (ta - 1,)
    waiting = (0, sa // 3 - 1)
    far = (2 * sa // 3 - 1, 2 * sa // 3)
    rest = [z for z in range(sa) if z not in waiting]
    near = [z for z in range(sa) if z not in far]
    zeroth = lax.ppermute(to_zeroth, ("ta", "sa"), along_t(slabs, 1, waiting) + along_t(late, 0, far))
    first = lax.ppermute(to_first, ("ta", "sa"), along_z(slabs[:-1], range(sa)) + along_z(last, near))
    second = lax.ppermute(to_second, ("ta", "sa"), along_t(slabs, 1, rest))
    third = lax.ppermute(
        to_third, ("ta", "sa"), along_t(slabs[:-2], 0, range(sa)) + along_t(late, 0, near) + along_z(last, far)
    )
    cores = lax.all_gather(to_core, "sa", axis_index_groups=[[i, i + 1] for i in range(0, sa, 2)])
    (local,) = call(
        functools.partial(local_kernel, (ta, sa)),
        [jax.ShapeDtypeStruct((2, 3, 4, columns, sites), F32)],
        (packed, clov, cores, zeroth, first, second),
        2500 * points,
    )
    result, partial = call(
        functools.partial(finish_kernel, (ta, sa)),
        [
            jax.ShapeDtypeStruct((2, 3, 4, columns, sites), BF16),
            jax.ShapeDtypeStruct((2, vectors.shape[2], 4 * columns), F32),
        ],
        (local, packed, third, vectors),
        500 * points,
    )
    perambulator, result = sum_over_blocks(partial, result, sa)
    return result.reshape(source_field.shape), perambulator[:, None]


def solution(mesh):
    in_specs = (
        P(None, None, None, None, "ta", "sa", None),
        P(None, None, None, None, "ta", "sa", None),
        P(None, None, None, None, "ta", "sa", None),
        P(None, None, None, "ta", "sa", None),
    )
    out_specs = (P(None, None, None, None, "ta", "sa", None), P(None, "ta", None, None))
    return jax.shard_map(shards, mesh=mesh, in_specs=in_specs, out_specs=out_specs, check_vma=False)
```

```python
import functools

import jax
import jax.numpy as jnp
from jax import lax
from jax.experimental import pallas as pl
from jax.experimental.pallas import tpu as pltpu
from jax.sharding import PartitionSpec as P

KAPPA = 0.125
ROWS = 16
LINK_ROWS = 72
F32 = jnp.float32
BF16 = jnp.bfloat16


def add(a, b):
    return (a[0] + b[0], a[1] + b[1])


def sub(a, b):
    return (a[0] - b[0], a[1] - b[1])


def neg(a):
    return (-a[0], -a[1])


def times_i(a):
    return (-a[1], a[0])


def spin(direction, w):
    if direction == 0:
        return [neg(times_i(w[1])), neg(times_i(w[0]))]
    if direction == 1:
        return [neg(w[1]), w[0]]
    if direction == 2:
        return [neg(times_i(w[0])), times_i(w[1])]
    return [w[0], w[1]]


def spin_dagger(direction, w):
    if direction == 0:
        return [times_i(w[1]), times_i(w[0])]
    if direction == 1:
        return [w[1], neg(w[0])]
    if direction == 2:
        return [times_i(w[0]), neg(times_i(w[1]))]
    return [w[0], w[1]]


def rounded(a):
    return (a[0].astype(BF16).astype(F32), a[1].astype(BF16).astype(F32))


def load_field(ref, rows, spins):
    return [
        [(ref[0, c, s, rows, :].astype(F32), ref[1, c, s, rows, :].astype(F32)) for s in range(spins)]
        for c in range(3)
    ]


class Field:
    def __init__(self, packed):
        self.packed, self.shape = packed, (2, 3, 4, (packed.shape[0] - LINK_ROWS) // 24, packed.shape[1])

    def __getitem__(self, at):
        q, c, s, rows, _ = at
        return self.packed[pl.ds(((q * 3 + c) * 4 + s) * self.shape[3] + rows.start, rows.size), :]


def load_links(packed, *directions):
    block = packed[pl.ds(packed.shape[0] - LINK_ROWS, LINK_ROWS), :].astype(F32)

    def row(q, a, b, direction):
        at = ((q * 3 + a) * 3 + b) * 4 + direction
        return block[at : at + 1, :]

    return [
        [[(row(0, a, b, direction), row(1, a, b, direction)) for b in range(3)] for a in range(3)]
        for direction in directions
    ]


def load_matrix(ref, which):
    tiles = [[[ref[q, a, b, :, :].astype(F32) for b in range(3)] for a in range(3)] for q in range(2)]
    return [
        [(tiles[0][a][b][which : which + 1, :], tiles[1][a][b][which : which + 1, :]) for b in range(3)]
        for a in range(3)
    ]


def color_row(matrix, part, a, s, dagger):
    re = im = None
    for b in range(3):
        x_re, x_im = part[b][s]
        if dagger:
            m_re, m_im = matrix[b][a]
            terms = (m_re * x_re + m_im * x_im, m_re * x_im - m_im * x_re)
        else:
            m_re, m_im = matrix[a][b]
            terms = (m_re * x_re - m_im * x_im, m_re * x_im + m_im * x_re)
        re = terms[0] if re is None else re + terms[0]
        im = terms[1] if im is None else im + terms[1]
    return (re, im)


def half(field, direction, plus):
    out = []
    for c in range(3):
        turned = spin(direction, [field[c][2], field[c][3]])
        out.append([(add if plus else sub)(field[c][s], turned[s]) for s in range(2)])
    return out


def knot(ta_size, sa_size):
    me, z = lax.axis_index("ta"), lax.axis_index("sa")
    far = (z == 2 * sa_size // 3 - 1) | (z == 2 * sa_size // 3)
    return far & (me >= ta_size - 2), far & (me == ta_size - 1)


def edge_kernel(sizes, packed, to_core, to_zeroth, to_first, to_second, to_third):
    src = Field(packed)
    columns = src.shape[3]
    link_z, link_t = load_links(packed, 2, 3)
    me = lax.axis_index("ta")
    even_z = lax.axis_index("sa") % 2 == 0
    even_t = me % 2 == 0
    late, last = knot(*sizes)
    for at in range(0, columns, ROWS):
        rows = pl.ds(at, ROWS)
        field = load_field(src, rows, 4)
        minus_z, minus_t = half(field, 2, False), half(field, 3, False)
        plus_z, plus_t = half(field, 2, True), half(field, 3, True)
        for a in range(3):
            for s in range(2):
                back_z = color_row(link_z, plus_z, a, s, True)
                back_t = color_row(link_t, plus_t, a, s, True)
                for q in range(2):
                    to_core[q, a, s, rows, :] = jnp.where(even_z, back_z[q], minus_z[a][s][q]).astype(BF16)
                    chip = jnp.where(even_z, minus_z[a][s][q], back_z[q])
                    even = jnp.where(even_t, back_t[q], minus_t[a][s][q])
                    odd = jnp.where(even_t, minus_t[a][s][q], back_t[q])
                    to_zeroth[q, a, s, rows, :] = jnp.where(late, even, odd).astype(BF16)
                    to_first[q, a, s, rows, :] = chip.astype(BF16)
                    to_second[q, a, s, rows, :] = odd.astype(BF16)
                    to_third[q, a, s, rows, :] = jnp.where(last, chip, even).astype(BF16)


def shift_sites(x, direction, ahead):
    lane = lax.broadcasted_iota(jnp.int32, x.shape, 1)
    if direction == 1:
        return pltpu.roll(x, 120 if ahead else 8, 1)
    if ahead:
        return jnp.where(lane % 8 == 7, pltpu.roll(x, 7, 1), pltpu.roll(x, 127, 1))
    return jnp.where(lane % 8 == 0, pltpu.roll(x, 121, 1), pltpu.roll(x, 1, 1))


def add_to(hop, a, values):
    for s, v in enumerate(values):
        hop[a][s] = v if hop[a][s] is None else add(hop[a][s], v)


def place_on_mesh(ta_size):
    me, core = lax.axis_index("ta"), lax.axis_index("sa") % 2
    ahead_sign = jnp.where(me == ta_size - 1, -1.0, 1.0).astype(F32)
    behind_sign = jnp.where(me == 0, -1.0, 1.0).astype(F32)
    return core, me % 2, ahead_sign, behind_sign


def chosen_matrix(first, a, b):
    return [[tuple(jnp.where(first, p, q) for p, q in zip(v, w)) for v, w in zip(x, y)] for x, y in zip(a, b)]


def add_swapped(hop, link, part, forward, turn, forward_sign=None, backward_sign=None):
    for a in range(3):
        upper, signed = [], []
        for s in range(2):
            w, g = color_row(link, part, a, s, False), part[a][s]
            if forward_sign is not None:
                w = (w[0] * forward_sign, w[1] * forward_sign)
                g = (g[0] * backward_sign, g[1] * backward_sign)
            upper.append(tuple(jnp.where(forward, p, q) for p, q in zip(w, g)))
            signed.append(tuple(jnp.where(forward, -p, q) for p, q in zip(w, g)))
        add_to(hop, a, upper + turn(signed))


def turned_z(w):
    return spin_dagger(2, w)


def turned_t(w):
    return spin_dagger(3, w)


def turned_either(along_t, w):
    return [
        tuple(jnp.where(along_t, p, q) for p, q in zip(v, u)) for v, u in zip(turned_t(w), turned_z(w))
    ]


def local_kernel(sizes, packed, clover, cores, zeroth, first, second, out):
    src = Field(packed)
    columns = src.shape[3]
    core, odd_t, ahead_sign, behind_sign = place_on_mesh(sizes[0])
    late, _ = knot(*sizes)
    link = load_links(packed, 0, 1, 2, 3)
    forward_zeroth = jnp.where(late, 1 - odd_t, odd_t) == 1
    clov = [load_matrix(clover, 0), load_matrix(clover, 1)]
    for at in range(0, columns, ROWS):
        rows = pl.ds(at, ROWS)
        field = load_field(src, rows, 4)
        hop = [[None] * 4 for _ in range(3)]
        for direction in range(2):
            minus = half(field, direction, False)
            ahead = [
                [tuple(shift_sites(v, direction, True) for v in rounded(minus[c][s])) for s in range(2)]
                for c in range(3)
            ]
            plus = half(field, direction, True)
            for a in range(3):
                w = [color_row(link[direction], ahead, a, s, False) for s in range(2)]
                g = [
                    tuple(
                        shift_sites(v, direction, False)
                        for v in rounded(color_row(link[direction], plus, a, s, True))
                    )
                    for s in range(2)
                ]
                upper = [add(w[s], g[s]) for s in range(2)]
                add_to(hop, a, upper + spin_dagger(direction, [sub(g[s], w[s]) for s in range(2)]))
        add_swapped(hop, link[2], load_field(cores.at[1 - core], rows, 2), core == 0, turned_z)
        add_swapped(hop, link[2], load_field(first, rows, 2), core == 1, turned_z)
        add_swapped(hop, link[3], load_field(second, rows, 2), odd_t == 1, turned_t, ahead_sign, behind_sign)
        add_swapped(hop, link[3], load_field(zeroth, rows, 2), forward_zeroth, turned_t, ahead_sign, behind_sign)
        for a in range(3):
            for s in range(4):
                own = add(field[a][s], color_row(clov[s // 2], field, a, s, False))
                for q in range(2):
                    out[q, a, s, rows, :] = own[q] - KAPPA * hop[a][s][q]


def finish_kernel(sizes, local, packed, third, vectors, result, partial):
    columns = local.shape[3]
    core, odd_t, _, _ = place_on_mesh(sizes[0])
    _, last = knot(*sizes)
    link = chosen_matrix(last, *load_links(packed, 2, 3))
    forward = jnp.where(last, core, 1 - odd_t) == 1
    turn = functools.partial(turned_either, jnp.logical_not(last))
    for at in range(0, columns, ROWS):
        rows = pl.ds(at, ROWS)
        hop = [[None] * 4 for _ in range(3)]
        add_swapped(hop, link, load_field(third, rows, 2), forward, turn)
        for a in range(3):
            for s in range(4):
                for q in range(2):
                    value = local[q, a, s, rows, :] - KAPPA * hop[a][s][q]
                    result[q, a, s, rows, :] = value.astype(BF16)
    total = None
    contract = (((1,), (1,)), ((), ()))
    for c in range(3):
        left_re = vectors[0, c]
        left_im = vectors[1, c]
        for q in range(2):
            right = result[q, c].reshape(4 * columns, result.shape[4])
            left = [left_re, -left_im] if q == 0 else [left_im, left_re]
            term = lax.dot_general(jnp.concatenate(left, axis=0), right, contract, preferred_element_type=F32)
            total = term if total is None else total + term
    partial[...] = total.reshape(partial.shape)


def copy_kernel(src, out):
    out[...] = src[...]


def call(body, outs, operands, flops, in_specs=None, scratch_shapes=()):
    vmem = pl.BlockSpec(memory_space=pltpu.VMEM)
    moved = sum(x.size * x.dtype.itemsize for x in list(outs) + list(operands))
    return pl.pallas_call(
        body,
        out_shape=outs,
        in_specs=in_specs or [vmem] * len(operands),
        out_specs=[vmem] * len(outs),
        scratch_shapes=scratch_shapes,
        compiler_params=pltpu.CompilerParams(vmem_limit_bytes=32 * 2**20),
        cost_estimate=pl.CostEstimate(flops=flops, bytes_accessed=moved, transcendentals=0),
    )(*operands)


def gathered_sum(x, groups):
    both = lax.all_gather(x, "sa", axis_index_groups=groups).astype(F32)
    return lax.reduce_precision(both[0] + both[1], 8, 7).astype(BF16)


def sum_over_blocks(partial, result, size):
    plane = 8
    planes = size // plane
    cores = [[i, i + 1] for i in range(0, size, 2)]
    starts = range(0, size, plane)
    even = [[z + 4 * p + c, z + 4 * p + 2 + c] for z in starts for p in range(2) for c in range(2)]
    odd = [[z + 2 + c, z + 4 + c] for z in starts for c in range(2)]
    odd += [[z + c, z + 6 + c] for z in starts for c in range(2)]
    row = [[z + 2 * x + c for x in range(4)] for z in starts for c in range(2)]
    s = gathered_sum(partial, cores)
    pairs = []
    for i in range(size):
        z, r = divmod(i, plane)
        step = 1 if i % 2 else planes - 1
        pairs.append((i, ((z + step) % planes) * plane + r))
    other = lax.ppermute(s, "sa", pairs)
    (result,) = call(copy_kernel, [jax.ShapeDtypeStruct(result.shape, BF16)], (result,), result.size)
    other, result = lax.optimization_barrier((other, result))
    other = lax.all_gather(other, "sa", axis_index_groups=cores)
    z = lax.axis_index("sa") // plane
    own, nxt, last = s.astype(F32), other[0].astype(F32), other[1].astype(F32)
    first = jnp.where(z == 0, own, jnp.where(z == 1, last, nxt))
    second = jnp.where(z == 0, nxt, jnp.where(z == 1, own, last))
    third = jnp.where(z == 0, last, jnp.where(z == 1, nxt, own))
    s = lax.reduce_precision(first + second + third, 8, 7).astype(BF16)
    four = lax.all_to_all(jnp.broadcast_to(s[None], (4,) + s.shape), "sa", 0, 0, axis_index_groups=row).astype(F32)
    return (four[0] + four[1]) + (four[2] + four[3]), result


def shards(source_field, gauge_links, clover, eigenvectors):
    sites = source_field.shape[-1]
    columns = source_field.shape[3]
    ta, sa = lax.axis_size("ta"), lax.axis_size("sa")
    src = source_field.reshape(2, 3, 4, columns, sites)
    links = gauge_links.reshape(2, 4, 3, 3, sites).transpose(0, 2, 3, 1, 4)
    clov = clover.reshape(2, 2, 3, 3, sites).transpose(0, 2, 3, 1, 4)
    vectors = eigenvectors.reshape(2, 3, eigenvectors.shape[2], sites)
    half_shape = jax.ShapeDtypeStruct((2, 3, 2, columns, sites), BF16)
    points = columns * sites

    packed = jnp.concatenate([src.reshape(-1, sites), links.reshape(-1, sites)])
    to_core, to_zeroth, to_first, to_second, to_third = call(
        functools.partial(edge_kernel, (ta, sa)),
        [half_shape] * 5,
        (packed,),
        500 * points,
    )

    def place(t, z):
        return (t % ta) * sa + z % sa

    def along_z(slabs, blocks):
        return [(place(t, z), place(t, z + (1 if z % 2 else -1))) for t in slabs for z in blocks]

    def along_t(slabs, parity, blocks):
        return [(place(t, z), place(t + (1 if t % 2 == parity else -1), z)) for t in slabs for z in blocks]

    slabs, late, last = range(ta), (ta - 2, ta - 1), (ta - 1,)
    ends = (0, ta - 1)
    waiting = (0, sa // 3 - 1)
    far = (2 * sa // 3 - 1, 2 * sa // 3)
    rest = [z for z in range(sa) if z not in waiting]
    near = [z for z in range(sa) if z not in far]
    zeroth = lax.ppermute(to_zeroth, ("ta", "sa"), along_t(slabs[1:-1], 1, waiting) + along_t(ends, 1, waiting[1:]) + along_t(late, 0, far))
    first = lax.ppermute(to_first, ("ta", "sa"), along_z(slabs[:-1], range(sa)) + along_z(last, near))
    second = lax.ppermute(to_second, ("ta", "sa"), along_t(slabs, 1, rest) + along_t(ends, 1, waiting[:1]))
    third = lax.ppermute(
        to_third, ("ta", "sa"), along_t(slabs[:-2], 0, range(sa)) + along_t(late, 0, near) + along_z(last, far)
    )
    cores = lax.all_gather(to_core, "sa", axis_index_groups=[[i, i + 1] for i in range(0, sa, 2)])
    (local,) = call(
        functools.partial(local_kernel, (ta, sa)),
        [jax.ShapeDtypeStruct((2, 3, 4, columns, sites), F32)],
        (packed, clov, cores, zeroth, first, second),
        2500 * points,
    )
    result, partial = call(
        functools.partial(finish_kernel, (ta, sa)),
        [
            jax.ShapeDtypeStruct((2, 3, 4, columns, sites), BF16),
            jax.ShapeDtypeStruct((2, vectors.shape[2], 4 * columns), F32),
        ],
        (local, packed, third, vectors),
        500 * points,
    )
    perambulator, result = sum_over_blocks(partial, result, sa)
    return result.reshape(source_field.shape), perambulator[:, None]


def solution(mesh):
    in_specs = (
        P(None, None, None, None, "ta", "sa", None),
        P(None, None, None, None, "ta", "sa", None),
        P(None, None, None, None, "ta", "sa", None),
        P(None, None, None, "ta", "sa", None),
    )
    out_specs = (P(None, None, None, None, "ta", "sa", None), P(None, "ta", None, None))
    return jax.shard_map(shards, mesh=mesh, in_specs=in_specs, out_specs=out_specs, check_vma=False)
```
